32 devices in a mesh: groups: 2 (over y), inst: 8 (over z, x), tp: 2 (over core).
Axes of the slice: x: 2, y: 2, z: 4, core: 2. Of those that a mesh axis runs over, the one named last changes fastest.
Arguments:
- source_cache: bfloat16 [16, 6, 4, 2, 128, 128], P(('groups', 'inst'), None, None, None, 'tp'), parts along dimension 0, may hold values from -18 to 18
- block_table: int32 [16, 6], P(('groups', 'inst')), parts along dimension 0, may hold values from 0 to 5, each once within a row
- lengths: int32 [16, 6], P('groups'), parts along dimension 0, may hold values from 16 to 128, as said below
- target_map: int32 [16, 6], P('groups'), parts along dimension 0, may hold values from 0 to 7, as said below
- queries: bfloat16 [6, 16, 6, 64, 128], P(None, ('groups', 'inst'), None, 'tp'), parts along dimension 1, may hold values from -50 to 50
- fresh_cache: bfloat16 [6, 16, 6, 4, 2, 128], P(None, ('groups', 'inst'), None, 'tp'), parts along dimension 1, may hold values from -6 to 6
- positions: int32 [16, 6], P(('groups', 'inst')), parts along dimension 0, may hold values from 256 to 4095
Outputs:
- scales: bfloat16 [16, 6, 4, 2], P(('groups', 'inst'), None, 'tp'), parts along dimension 0
- attended: bfloat16 [6, 16, 6, 64, 128], P(None, ('groups', 'inst'), None, 'tp'), parts along dimension 1
The draws below stay inside these ranges and needn't reach their ends.
There are 2 independent parts, one for each index of `groups`. The reference program is written for one: setup_inputs(seed, part) draws one part's arguments, and reference() takes and returns one part's arrays. A program takes and returns all parts, laid end to end along the dimension named above; each array names one. Nothing has to cross between parts.
Inputs may be any that keep to these rules, and one draw needn't show every extreme that they name: `target_map`: for each request number j the sources go to distinct targets; a source never sends to itself and sends its 6 requests to distinct targets. `lengths`: some request has exactly 128 tokens.
All inputs are finite; a program needn't handle non-finite values.
Results may differ from the reference program's by a relative error of at most 0.0062.
Values may be sent and summed in bfloat16 or wider, within the bound.
A program may use at most 128 MiB of HBM per device.

```python
import math
import jax
import jax.numpy as jnp
from jax import lax

QH = 64
KVH = 4
HD = 128
PAGE = 128
STEPS = 6
INSTANCES = 8
REQ = 6


def route_plan(key):
    key = jax.random.fold_in(key, 17)
    first, second, third = jax.random.split(key, 3)
    order = jax.random.permutation(first, INSTANCES).astype(jnp.int32)
    rank = jnp.argsort(order).astype(jnp.int32)
    shifts = jax.random.permutation(second, INSTANCES - 1)[:REQ].astype(jnp.int32) + 1
    targets = order[(rank[:, None] + shifts[None, :]) % INSTANCES]
    levels = jax.random.randint(third, (INSTANCES,), 0, 3)
    levels = levels.at[order[0]].set(0)
    return (targets.astype(jnp.int32), levels, order)


def draw_target_map(key, part):
    return route_plan(key)[0]


def draw_lengths(key, part):
    targets, levels, order = route_plan(key)
    key = jax.random.fold_in(key, 29)
    ceiling_of = jnp.where(levels == 0, PAGE, jnp.where(levels == 1, PAGE // 2, PAGE // 4)).astype(jnp.int32)
    ceiling = ceiling_of[targets]
    drawn = jax.random.randint(key, (INSTANCES, REQ), ceiling // 2, ceiling + 1)
    first_slot = jnp.arange(REQ, dtype=jnp.int32)[None, :] == 0
    return jnp.where((targets == order[0]) & first_slot, PAGE, drawn).astype(jnp.int32)


def draw_source_cache(key, part):
    key = jax.random.fold_in(key, 3)
    first, second = jax.random.split(key, 2)
    shape = (INSTANCES, REQ, KVH, 2, PAGE, HD)
    spread = jnp.exp(jax.random.uniform(second, (INSTANCES, REQ, KVH, 2, PAGE, 1), minval=math.log(0.3), maxval=math.log(3.0)))
    values = jax.random.normal(first, shape) * spread
    return jnp.clip(values, -18.0, 18.0).astype(jnp.bfloat16)


def draw_fresh_cache(key, part):
    key = jax.random.fold_in(key, 5)
    first, second = jax.random.split(key, 2)
    shape = (STEPS, INSTANCES, REQ, KVH, HD)
    values = jnp.clip(jax.random.normal(second, shape), -6.0, 6.0)
    fresh_keys = jnp.clip(jax.random.normal(first, shape), -6.0, 6.0)
    return jnp.stack([fresh_keys, values], axis=4).astype(jnp.bfloat16)


def draw_queries(key, part):
    key = jax.random.fold_in(key, 7)
    shape = (STEPS, INSTANCES, REQ, QH, HD)
    values = jnp.clip(jax.random.normal(key, shape), -6.0, 6.0)
    return values.astype(jnp.bfloat16)


def touch_ends(values, key, low, high):
    spot = [jax.random.randint(jax.random.fold_in(key, axis), (), 0, length) for axis, length in enumerate(values.shape)]
    widest = values.shape.index(max(values.shape))
    next_to = spot[:widest] + [(spot[widest] + 1) % values.shape[widest]] + spot[widest + 1:]
    return values.at[tuple(spot)].set(low).at[tuple(next_to)].set(high)


def setup_inputs(seed: int = 0, part: int = 0) -> dict:
    arg_keys = jax.random.split(jax.random.key(seed), 8)
    part_keys = jax.random.split(jax.random.fold_in(arg_keys[7], part), 8)
    return {
        "source_cache": draw_source_cache(jax.random.fold_in(jax.random.fold_in(arg_keys[7], part), 71), part),
        "block_table": jax.vmap(lambda own: jax.random.permutation(own, REQ))(jax.random.split(part_keys[1], INSTANCES)).reshape((INSTANCES, REQ)).astype(jnp.int32),
        "lengths": draw_lengths(jax.random.fold_in(jax.random.fold_in(arg_keys[7], part), 71), part),
        "target_map": draw_target_map(jax.random.fold_in(jax.random.fold_in(arg_keys[7], part), 71), part),
        "queries": draw_queries(jax.random.fold_in(jax.random.fold_in(arg_keys[7], part), 71), part),
        "fresh_cache": draw_fresh_cache(jax.random.fold_in(jax.random.fold_in(arg_keys[7], part), 71), part),
        "positions": touch_ends(jax.random.randint(part_keys[6], (INSTANCES, REQ), 256, 4096), jax.random.fold_in(part_keys[6], 1), 256, 4095).astype(jnp.int32),
    }


ROPE_BASE = 1000000.0
HIGHEST = lax.Precision.HIGHEST

def sylvester(order):
    indices = jnp.arange(order, dtype=jnp.int32)
    common = jnp.bitwise_and(indices[:, None], indices[None, :])
    parity = jnp.zeros((order, order), dtype=jnp.int32)
    for level in range(order.bit_length() - 1):
        parity = parity + common // 2 ** level % 2
    return (1 - 2 * (parity % 2)).astype(jnp.bfloat16)

def rotary(vectors, places):
    width = vectors.shape[-1]
    half = width // 2
    exponents = jnp.arange(half, dtype=jnp.float32) * (2.0 / width)
    frequency = jnp.power(jnp.float32(ROPE_BASE), -exponents)
    angles = places.astype(jnp.float32)[..., None] * frequency
    cosine = jnp.cos(angles)
    sine = jnp.sin(angles)
    first = vectors[..., :half]
    second = vectors[..., half:]
    return jnp.concatenate([first * cosine - second * sine, second * cosine + first * sine], axis=-1)

def unchanged(values):
    return values

def decode_step(query_cache, query_fresh, cache_keys, cache_values, valid, fresh_keys, fresh_values, finish):
    factor = 1.0 / math.sqrt(query_cache.shape[-1])
    cached = jnp.einsum('rkgd,rkpd->rkgp', query_cache, cache_keys, precision=HIGHEST) * factor
    cached = jnp.where(valid[:, None, None, :], cached, -jnp.inf)
    recent = jnp.einsum('rkgd,rkud->rkgu', query_fresh, fresh_keys, precision=HIGHEST) * factor
    top = jnp.maximum(lax.optimization_barrier(jnp.max(cached, axis=-1)), lax.optimization_barrier(jnp.max(recent, axis=-1)))[..., None]
    cached_weight = jnp.exp(cached - top)
    recent_weight = jnp.exp(recent - top)
    total = lax.optimization_barrier(jnp.sum(cached_weight, axis=-1)) + lax.optimization_barrier(jnp.sum(recent_weight, axis=-1))
    mixed = finish(jnp.einsum('rkgp,rkpd->rkgd', cached_weight, cache_values, precision=HIGHEST))
    mixed = mixed + jnp.einsum('rkgu,rkud->rkgd', recent_weight, fresh_values, precision=HIGHEST)
    return mixed / total[..., None]

def reference(source_cache, block_table, lengths, target_map, queries, fresh_cache, positions):
    hadamard = sylvester(HD)
    hadamard_wide = hadamard.astype(jnp.float32)
    inv_root = 1.0 / math.sqrt(HD)
    tokens = jnp.arange(PAGE, dtype=jnp.int32)
    group = QH // KVH

    def quantize(inputs):
        cache_rows, table_row, length_row = inputs
        pages = cache_rows[table_row]
        rotated = jnp.dot(pages.reshape(-1, HD), hadamard, preferred_element_type=jnp.float32) * inv_root
        rotated = rotated.reshape(pages.shape)
        valid = tokens[None, :] < length_row[:, None]
        rotated = jnp.where(valid[:, None, None, :, None], rotated, 0.0)
        block_max = lax.optimization_barrier(jnp.max(jnp.abs(rotated), axis=(3, 4)))
        block_scale = (block_max + 1e-06).astype(jnp.bfloat16)
        quantized = (rotated / block_scale.astype(jnp.float32)[..., None, None]).astype(jnp.bfloat16)
        return (quantized, block_scale)
    quantized, block_scale = lax.map(quantize, (source_cache, block_table, lengths))
    slots = jnp.arange(REQ, dtype=jnp.int32)[None, :]
    migrated = jnp.zeros_like(quantized).at[target_map, slots].set(quantized)
    scales = jnp.zeros_like(block_scale).at[target_map, slots].set(block_scale)
    sources = jnp.arange(INSTANCES, dtype=jnp.int32)[:, None] + jnp.zeros_like(target_map)
    source_of = jnp.zeros_like(target_map).at[target_map, slots].set(sources)
    valid_len = lengths[source_of, slots]

    def decode(inputs):
        pages, page_scale, length_row, query_rows, fresh_rows, place_row = inputs
        restored = pages.astype(jnp.float32) * page_scale.astype(jnp.float32)[..., None, None]
        restored = jnp.einsum('rkepd,dc->rkepc', restored, hadamard_wide, precision=HIGHEST) * inv_root
        valid = tokens[None, :] < length_row[:, None]
        places = place_row[None, :] + jnp.arange(STEPS, dtype=jnp.int32)[:, None]
        fresh_keys = rotary(fresh_rows[:, :, :, 0].astype(jnp.float32), places[:, :, None])
        fresh_keys = jnp.transpose(fresh_keys, (1, 2, 0, 3))
        fresh_values = jnp.transpose(fresh_rows[:, :, :, 1].astype(jnp.float32), (1, 2, 0, 3))
        outputs = []
        for step in range(STEPS):
            query_rot = rotary(query_rows[step].astype(jnp.float32), places[step][:, None])
            query_rot = query_rot.reshape(REQ, KVH, group, HD)
            mixed = decode_step(query_rot, query_rot, restored[:, :, 0], restored[:, :, 1], valid, fresh_keys[:, :, :step + 1], fresh_values[:, :, :step + 1], unchanged)
            outputs.append(mixed.reshape(REQ, QH, HD))
        return jnp.stack(outputs).astype(jnp.bfloat16)
    attended = lax.map(decode, (migrated, scales, valid_len, jnp.swapaxes(queries, 0, 1), jnp.swapaxes(fresh_cache, 0, 1), positions))
    attended = jnp.swapaxes(attended, 0, 1)
    return (scales, attended)
```

```python
import functools
import math

import jax
import jax.numpy as jnp
from jax import lax
from jax.experimental import pallas as pl
from jax.experimental.pallas import tpu as pltpu
from jax.sharding import PartitionSpec as P

ROPE_BASE = 1000000.0
HIGHEST = lax.Precision.HIGHEST
MESH = pl.DeviceIdType.MESH
F32 = jnp.float32
BF16 = jnp.bfloat16


def sylvester(order):
    rows = lax.broadcasted_iota(jnp.int32, (order, order), 0)
    columns = lax.broadcasted_iota(jnp.int32, (order, order), 1)
    common = jnp.bitwise_and(rows, columns)
    parity = jnp.zeros((order, order), dtype=jnp.int32)
    for level in range(order.bit_length() - 1):
        parity = parity + jnp.bitwise_and(lax.shift_right_logical(common, level), 1)
    return (1 - 2 * jnp.bitwise_and(parity, 1)).astype(F32).astype(BF16)


def split(values):
    high = values.astype(BF16)
    low = (values - high.astype(F32)).astype(BF16)
    return high, low


def dot(a, b):
    return jnp.dot(a, b, preferred_element_type=F32)


def dot_t(a, b, precision=None):
    return lax.dot_general(
        a, b, (((1,), (1,)), ((), ())), precision=precision, preferred_element_type=F32
    )


def kernel(
    n,
    table_ref,
    length_ref,
    map_ref,
    cache_ref,
    query_ref,
    fresh_ref,
    turn_ref,
    out_ref,
    scale_ref,
    had,
    other,
    quant,
    scale,
    ask,
    asked,
    turns,
    turned,
    reply,
    replied,
    swap_sem,
    ask_send,
    ask_recv,
    turn_send,
    turn_recv,
    reply_send,
    reply_recv,
):
    group = lax.axis_index("groups")
    me = lax.axis_index("inst")
    rank = lax.axis_index("tp")
    steps, _, requests, query_heads, width = query_ref.shape
    heads = cache_ref.shape[1] // 2
    half = cache_ref.shape[3]
    share = query_heads // heads
    rows = steps * share
    asks = heads * rows
    factor = 1.0 / math.sqrt(width)

    def after(d):
        return lax.rem(me + d, n)

    def before(d):
        return lax.rem(me + n - d, n)

    barrier = pltpu.get_barrier_semaphore()

    pl.semaphore_signal(barrier, inc=1, device_id=(group, me, 1 - rank), device_id_type=MESH)

    @pl.loop(1, n)
    def _(d):
        pl.semaphore_signal(barrier, inc=1, device_id=(group, after(d), rank), device_id_type=MESH)

    had[...] = sylvester(width)
    pl.semaphore_wait(barrier, n)

    swap = pltpu.make_async_remote_copy(
        src_ref=cache_ref.at[:, pl.ds((1 - rank) * heads, heads)],
        dst_ref=other,
        send_sem=swap_sem.at[0],
        recv_sem=swap_sem.at[1],
        device_id=(group, me, 1 - rank),
        device_id_type=MESH,
    )
    swap.start()

    def ask_copy(d, slot, target):
        return pltpu.make_async_remote_copy(
            src_ref=ask.at[after(d)],
            dst_ref=asked.at[slot],
            send_sem=ask_send.at[d],
            recv_sem=ask_recv.at[d],
            device_id=(group, target, rank),
            device_id_type=MESH,
        )

    def turn_copy(d, slot, target):
        return pltpu.make_async_remote_copy(
            src_ref=turns.at[after(d)],
            dst_ref=turned.at[slot],
            send_sem=turn_send.at[d],
            recv_sem=turn_recv.at[d],
            device_id=(group, target, rank),
            device_id_type=MESH,
        )

    def reply_copy(d, slot, target):
        return pltpu.make_async_remote_copy(
            src_ref=reply.at[before(d)],
            dst_ref=replied.at[slot],
            send_sem=reply_send.at[d],
            recv_sem=reply_recv.at[d],
            device_id=(group, target, rank),
            device_id_type=MESH,
        )

    @pl.loop(1, n)
    def _(d):
        source = after(d)
        chosen = jnp.int32(0)
        for j in range(requests):
            chosen = jnp.maximum(chosen, jnp.where(map_ref[source, j] == me, j, 0))
        for g in range(heads):
            for u in range(steps):
                ask[source, pl.ds(g * rows + u * share, share), :] = query_ref[
                    u, 0, chosen, pl.ds(g * share, share), :
                ]
        ask[source, pl.ds(asks, 32), :] = fresh_ref[chosen]
        turns[source] = turn_ref[chosen]
        turn_copy(d, me, source).start()
        ask_copy(d, me, source).start()

    swap.wait_recv()

    token = lax.broadcasted_iota(jnp.int32, (2 * half, width), 0)
    token = jnp.where(token < half, token + rank * half, token - half + (1 - rank) * half)
    line = lax.broadcasted_iota(jnp.int32, (16, width), 0)

    @pl.loop(0, requests)
    def _(j):
        page = table_ref[0, j]
        keep = token < length_ref[me, j]
        signs = had[...]
        packed = jnp.zeros((16, width), F32)
        for g in range(heads):
            for e in range(2):
                values = jnp.concatenate(
                    [cache_ref[page, rank * heads + g, e], other[page, g, e]], axis=0
                )
                rotated = jnp.where(keep, dot(values, signs) * factor, 0.0)
                top = jnp.max(jnp.max(jnp.abs(rotated), axis=0, keepdims=True), axis=1, keepdims=True)
                block = (jnp.broadcast_to(top, (16, width)) + 1e-06).astype(BF16).astype(F32)
                packed = jnp.where(line == 2 * g + e, block, packed)
                quant[j, g, e] = (rotated / block[:1]).astype(BF16)
        scale[j] = packed

    lane = lax.broadcasted_iota(jnp.int32, (8, width), 1)
    row = lax.broadcasted_iota(jnp.int32, (rows, 8), 0)
    later = lax.broadcasted_iota(jnp.int32, (rows, 8), 1)
    open_ = later * share <= row
    column = lax.broadcasted_iota(jnp.int32, (rows, 2 * half), 1)
    column = jnp.where(column < half, column + rank * half, column - half + (1 - rank) * half)

    @pl.loop(1, n)
    def _(d):
        target = before(d)
        turn_copy(d, target, target).wait_recv()
        ask_copy(d, target, target).wait_recv()
        chosen = jnp.int32(0)
        for j in range(requests):
            chosen = jnp.maximum(chosen, jnp.where(map_ref[me, j] == target, j, 0))
        keep = column < length_ref[me, chosen]
        signs = had[...]
        packed = scale[chosen]
        turn = turned[target]
        flipped = pltpu.roll(turn, width // 2, 1)
        cosine = jnp.where(lane < width // 2, turn, flipped)
        sine = jnp.where(lane < width // 2, -flipped, turn)
        wide_cosine = jnp.concatenate(
            [jnp.broadcast_to(cosine[u : u + 1], (share, width)) for u in range(steps)], axis=0
        )
        wide_sine = jnp.concatenate(
            [jnp.broadcast_to(sine[u : u + 1], (share, width)) for u in range(steps)], axis=0
        )
        fresh = asked[target, pl.ds(asks, 32), :].astype(F32)
        for g in range(heads):
            query = asked[target, pl.ds(g * rows, rows), :].astype(F32)
            query = query * wide_cosine + pltpu.roll(query, width // 2, 1) * wide_sine
            key = fresh[16 * g : 16 * g + 8]
            key = key * cosine + pltpu.roll(key, width // 2, 1) * sine
            value = fresh[16 * g + 8 : 16 * g + 16]
            high, low = split(query)
            mixed_high, mixed_low = split(dot(high, signs) + dot(low, signs))
            keys = quant[chosen, g, 0]
            cached = dot_t(mixed_high, keys) + dot_t(mixed_low, keys)
            cached = cached * (packed[2 * g : 2 * g + 1] * (factor * factor))
            cached = jnp.where(keep, cached, -jnp.inf)
            recent = dot_t(query, key, HIGHEST) * factor
            recent = jnp.where(open_, recent, -jnp.inf)
            top = jnp.maximum(
                jnp.max(cached, axis=1, keepdims=True), jnp.max(recent, axis=1, keepdims=True)
            )
            cached = jnp.exp(cached - top)
            recent = jnp.exp(recent - top)
            total = jnp.sum(cached, axis=1, keepdims=True) + jnp.sum(recent, axis=1, keepdims=True)
            high, low = split(cached)
            values = quant[chosen, g, 1]
            mixed = (dot(high, values) + dot(low, values)) * (
                packed[2 * g + 1 : 2 * g + 2] * factor
            )
            high, low = split(mixed)
            mixed = dot(high, signs) + dot(low, signs)
            mixed = mixed + jnp.dot(recent, value, precision=HIGHEST, preferred_element_type=F32)
            reply[target, pl.ds(g * rows, rows), :] = (mixed / total).astype(BF16)
        reply[target, pl.ds(asks, 16), :] = packed.astype(BF16)
        reply_copy(d, me, target).start()

    @pl.loop(1, n)
    def _(d):
        source = after(d)
        reply_copy(d, source, source).wait_recv()

    @pl.loop(0, requests)
    def _(j):
        source = jnp.int32(0)
        for s in range(n):
            source = jnp.maximum(source, jnp.where(map_ref[s, j] == me, s, 0))
        for g in range(heads):
            for u in range(steps):
                out_ref[u, 0, j, pl.ds(g * share, share), :] = replied[
                    source, pl.ds(g * rows + u * share, share), :
                ]
        scale_ref[j] = replied[source, pl.ds(asks, 16), :]

    swap.wait_send()

    @pl.loop(1, n)
    def _(d):
        turn_copy(d, me, after(d)).wait_send()
        ask_copy(d, me, after(d)).wait_send()
        reply_copy(d, me, before(d)).wait_send()


def on_device(source_cache, block_table, lengths, target_map, queries, fresh_cache, positions):
    n = lax.axis_size("inst")
    _, requests, all_heads, pair, half, width = source_cache.shape
    steps = queries.shape[0]
    heads = fresh_cache.shape[3]
    asks = queries.shape[3] * steps
    exponents = jnp.arange(width // 2, dtype=F32) * (2.0 / width)
    frequency = jnp.power(F32(ROPE_BASE), -exponents)
    places = positions[0][:, None] + jnp.arange(8, dtype=jnp.int32)[None, :]
    angles = places.astype(F32)[..., None] * frequency
    turn = jnp.concatenate([jnp.cos(angles), jnp.sin(angles)], axis=-1)
    fresh = jnp.transpose(fresh_cache[:, 0], (1, 2, 3, 0, 4))
    fresh = jnp.pad(fresh, ((0, 0), (0, 0), (0, 0), (0, 8 - steps), (0, 0)))
    fresh = fresh.reshape(requests, heads * pair * 8, width)
    smem = pl.BlockSpec(memory_space=pltpu.SMEM)
    vmem = pl.BlockSpec(memory_space=pltpu.VMEM)
    dma = pltpu.SemaphoreType.DMA
    attended, scales = pl.pallas_call(
        functools.partial(kernel, n),
        out_shape=(
            jax.ShapeDtypeStruct(queries.shape, BF16),
            jax.ShapeDtypeStruct((requests, 16, width), BF16),
        ),
        in_specs=[smem] * 3 + [vmem] * 4,
        out_specs=(vmem, vmem),
        scratch_shapes=[
            pltpu.VMEM((width, width), BF16),
            pltpu.VMEM((requests, heads, pair, half, width), BF16),
            pltpu.VMEM((requests, heads, pair, 2 * half, width), BF16),
            pltpu.VMEM((requests, 16, width), F32),
            pltpu.VMEM((n, asks + 32, width), BF16),
            pltpu.VMEM((n, asks + 32, width), BF16),
            pltpu.VMEM((n, 8, width), F32),
            pltpu.VMEM((n, 8, width), F32),
            pltpu.VMEM((n, asks + 16, width), BF16),
            pltpu.VMEM((n, asks + 16, width), BF16),
            dma((2,)),
            dma((n,)),
            dma((n,)),
            dma((n,)),
            dma((n,)),
            dma((n,)),
            dma((n,)),
        ],
        compiler_params=pltpu.CompilerParams(
            collective_id=0, has_side_effects=True, vmem_limit_bytes=52 * 2**20
        ),
        cost_estimate=pl.CostEstimate(flops=10**9, bytes_accessed=4 * 10**6, transcendentals=10**5),
    )(block_table, lengths, target_map, source_cache[0], queries, fresh, turn)
    scales = scales[:, : heads * pair, 0].reshape(1, requests, heads, pair)
    return scales, attended


def solution(mesh):
    return jax.shard_map(
        on_device,
        mesh=mesh,
        in_specs=(
            P(("groups", "inst"), None, None, None, "tp", None),
            P(("groups", "inst"), None),
            P("groups", None),
            P("groups", None),
            P(None, ("groups", "inst"), None, "tp", None),
            P(None, ("groups", "inst"), None, "tp", None, None),
            P(("groups", "inst"), None),
        ),
        out_specs=(
            P(("groups", "inst"), None, "tp", None),
            P(None, ("groups", "inst"), None, "tp", None),
        ),
        check_vma=False,
    )
```

```python
import functools
import math

import jax
import jax.numpy as jnp
from jax import lax
from jax.experimental import pallas as pl
from jax.experimental.pallas import tpu as pltpu
from jax.sharding import PartitionSpec as P

ROPE_BASE = 1000000.0
MESH = pl.DeviceIdType.MESH
F32 = jnp.float32
BF16 = jnp.bfloat16


def sylvester(order):
    rows = lax.broadcasted_iota(jnp.int32, (order, order), 0)
    columns = lax.broadcasted_iota(jnp.int32, (order, order), 1)
    common = jnp.bitwise_and(rows, columns)
    parity = jnp.zeros((order, order), dtype=jnp.int32)
    for level in range(order.bit_length() - 1):
        parity = parity + jnp.bitwise_and(lax.shift_right_logical(common, level), 1)
    return (1 - 2 * jnp.bitwise_and(parity, 1)).astype(F32).astype(BF16)


def split(values):
    high = values.astype(BF16)
    low = (values - high.astype(F32)).astype(BF16)
    return high, low


def dot(a, b):
    return jnp.dot(a, b, preferred_element_type=F32)


def dot_t(a, b):
    return lax.dot_general(
        a, b, (((1,), (1,)), ((), ())), preferred_element_type=F32
    )


def kernel(
    n,
    table_ref,
    length_ref,
    map_ref,
    cache_ref,
    query_ref,
    fresh_ref,
    turn_ref,
    out_ref,
    scale_ref,
    had,
    own,
    other,
    quant,
    scale,
    ask,
    asked,
    turns,
    turned,
    reply,
    replied,
    swap_sem,
    ask_send,
    ask_recv,
    turn_send,
    turn_recv,
    reply_send,
    reply_recv,
):
    group = lax.axis_index("groups")
    me = lax.axis_index("inst")
    rank = lax.axis_index("tp")
    steps, _, requests, query_heads, width = query_ref.shape
    heads = cache_ref.shape[2] // 2
    half = cache_ref.shape[4]
    share = query_heads // heads
    rows = steps * share
    asks = heads * rows
    factor = 1.0 / math.sqrt(width)

    def after(d):
        return lax.rem(me + d, n)

    def before(d):
        return lax.rem(me + n - d, n)

    fetch = pltpu.make_async_copy(
        cache_ref.at[0, :, pl.ds(rank * heads, heads)], own, swap_sem.at[2]
    )
    fetch.start()
    barrier = pltpu.get_barrier_semaphore()

    pl.semaphore_signal(barrier, inc=1, device_id=(group, me, 1 - rank), device_id_type=MESH)

    @pl.loop(1, n)
    def _(d):
        pl.semaphore_signal(barrier, inc=1, device_id=(group, after(d), rank), device_id_type=MESH)

    had[...] = sylvester(width)
    pl.semaphore_wait(barrier, n)

    swap = pltpu.make_async_remote_copy(
        src_ref=cache_ref.at[0, :, pl.ds((1 - rank) * heads, heads)],
        dst_ref=other,
        send_sem=swap_sem.at[0],
        recv_sem=swap_sem.at[1],
        device_id=(group, me, 1 - rank),
        device_id_type=MESH,
    )
    swap.start()

    def ask_copy(d, slot, target):
        return pltpu.make_async_remote_copy(
            src_ref=ask.at[after(d)],
            dst_ref=asked.at[slot],
            send_sem=ask_send.at[d],
            recv_sem=ask_recv.at[d],
            device_id=(group, target, rank),
            device_id_type=MESH,
        )

    def turn_copy(d, slot, target):
        return pltpu.make_async_remote_copy(
            src_ref=turns.at[after(d)],
            dst_ref=turned.at[slot],
            send_sem=turn_send.at[d],
            recv_sem=turn_recv.at[d],
            device_id=(group, target, rank),
            device_id_type=MESH,
        )

    def reply_copy(d, slot, target):
        return pltpu.make_async_remote_copy(
            src_ref=reply.at[before(d)],
            dst_ref=replied.at[slot],
            send_sem=reply_send.at[d],
            recv_sem=reply_recv.at[d],
            device_id=(group, target, rank),
            device_id_type=MESH,
        )

    @pl.loop(1, n)
    def _(d):
        source = after(d)
        chosen = jnp.int32(0)
        for j in range(requests):
            chosen = jnp.maximum(chosen, jnp.where(map_ref[source, j] == me, j, 0))
        for g in range(heads):
            for u in range(steps):
                ask[source, pl.ds(g * rows + u * share, share), :] = query_ref[
                    u, 0, chosen, pl.ds(g * share, share), :
                ]
        ask[source, pl.ds(asks, 32), :] = fresh_ref[chosen]
        turns[source] = turn_ref[chosen]
        turn_copy(d, me, source).start()
        ask_copy(d, me, source).start()

    fetch.wait()
    swap.wait_recv()

    token = lax.broadcasted_iota(jnp.int32, (2 * half, width), 0)
    token = jnp.where(token < half, token + rank * half, token - half + (1 - rank) * half)
    line = lax.broadcasted_iota(jnp.int32, (16, width), 0)

    @pl.loop(0, requests)
    def _(j):
        page = table_ref[0, j]
        keep = token < length_ref[me, j]
        signs = had[...]
        packed = jnp.zeros((16, width), F32)
        for g in range(heads):
            for e in range(2):
                values = jnp.concatenate(
                    [own[page, g, e], other[page, g, e]], axis=0
                )
                rotated = jnp.where(keep, dot(values, signs) * factor, 0.0)
                top = jnp.max(jnp.max(jnp.abs(rotated), axis=0, keepdims=True), axis=1, keepdims=True)
                block = (jnp.broadcast_to(top, (16, width)) + 1e-06).astype(BF16).astype(F32)
                packed = jnp.where(line == 2 * g + e, block, packed)
                quant[j, g, e] = (rotated / block[:1]).astype(BF16)
        scale[j] = packed

    lane = lax.broadcasted_iota(jnp.int32, (8, width), 1)
    row = lax.broadcasted_iota(jnp.int32, (rows, width), 0)
    later = lax.broadcasted_iota(jnp.int32, (rows, width), 1)
    open_ = later * share <= row
    column = lax.broadcasted_iota(jnp.int32, (rows, 2 * half), 1)
    column = jnp.where(column < half, column + rank * half, column - half + (1 - rank) * half)

    def attend(target):
        chosen = jnp.int32(0)
        for j in range(requests):
            chosen = jnp.maximum(chosen, jnp.where(map_ref[me, j] == target, j, 0))
        keep = column < length_ref[me, chosen]
        signs = had[...]
        packed = scale[chosen]
        turn = turned[target]
        flipped = pltpu.roll(turn, width // 2, 1)
        cosine = jnp.where(lane < width // 2, turn, flipped)
        sine = jnp.where(lane < width // 2, -flipped, turn)

        def wide(values):
            blocks = [jnp.broadcast_to(values[u : u + 1], (share, width)) for u in range(steps)]
            return jnp.concatenate(blocks * heads, axis=0)

        fresh = asked[target, pl.ds(asks, 32), :].astype(F32)
        query = asked[target, pl.ds(0, asks), :].astype(F32)
        query = query * wide(cosine) + pltpu.roll(query, width // 2, 1) * wide(sine)
        high, low = split(query)
        query_high, query_low = split(dot(high, signs) + dot(low, signs))
        zeros = jnp.zeros((8, width), F32)
        blank = jnp.zeros((width - 16, width), BF16)
        results = []
        for g in range(heads):
            key = fresh[16 * g : 16 * g + 8]
            key = key * cosine + pltpu.roll(key, width // 2, 1) * sine
            high = key.astype(BF16).astype(F32)
            key = dot(jnp.concatenate([high, key - high], axis=0).astype(BF16), signs)
            key = key[:8] + key[8:]
            high = key.astype(BF16).astype(F32)
            key = jnp.concatenate([high, key - high], axis=0).astype(BF16)
            keys = jnp.concatenate([quant[chosen, g, 0], key, blank], axis=0)
            value = jnp.concatenate([fresh[16 * g + 8 : 16 * g + 16], zeros], axis=0).astype(BF16)
            value = jnp.concatenate([signs, value, blank], axis=0)
            mine = slice(g * rows, (g + 1) * rows)
            scores = dot_t(query_high[mine], keys) + dot_t(query_low[mine], keys)
            cached = scores[:, :width] * (packed[2 * g : 2 * g + 1] * (factor * factor))
            cached = jnp.where(keep, cached, -jnp.inf)
            recent = scores[:, width:]
            recent = (recent + pltpu.roll(recent, width - 8, 1)) * (factor * factor * factor)
            recent = jnp.where(open_, recent, -jnp.inf)
            top = jnp.max(jnp.maximum(cached, recent), axis=1, keepdims=True)
            cached = jnp.exp(cached - top).astype(BF16)
            recent = jnp.exp(recent - top).astype(BF16)
            total = jnp.sum(cached.astype(F32) + recent.astype(F32), axis=1, keepdims=True)
            mixed = dot(cached, quant[chosen, g, 1])
            mixed = (mixed * (packed[2 * g + 1 : 2 * g + 2] * factor)).astype(BF16)
            mixed = dot(jnp.concatenate([mixed, recent], axis=1), value)
            results.append((mixed / total).astype(BF16))
        results.append(packed.astype(BF16))
        return jnp.concatenate(results, axis=0)

    def serve(distances):
        for d in distances:
            turn_copy(d, before(d), before(d)).wait_recv()
            ask_copy(d, before(d), before(d)).wait_recv()
        results = [attend(before(d)) for d in distances]
        for d, result in zip(distances, results):
            reply[before(d)] = result
            reply_copy(d, me, before(d)).start()

    serve([1])

    @pl.loop(0, (n - 2) // 2)
    def _(pair):
        serve([2 + 2 * pair, 3 + 2 * pair])

    @pl.loop(1, n)
    def _(d):
        source = after(d)
        reply_copy(d, source, source).wait_recv()

    @pl.loop(0, requests)
    def _(j):
        source = jnp.int32(0)
        for s in range(n):
            source = jnp.maximum(source, jnp.where(map_ref[s, j] == me, s, 0))
        for g in range(heads):
            for u in range(steps):
                out_ref[u, 0, j, pl.ds(g * share, share), :] = replied[
                    source, pl.ds(g * rows + u * share, share), :
                ]
        scale_ref[j] = replied[source, pl.ds(asks, 16), :]

    swap.wait_send()

    @pl.loop(1, n)
    def _(d):
        turn_copy(d, me, after(d)).wait_send()
        ask_copy(d, me, after(d)).wait_send()
        reply_copy(d, me, before(d)).wait_send()


def on_device(source_cache, block_table, lengths, target_map, queries, fresh_cache, positions):
    n = lax.axis_size("inst")
    _, requests, all_heads, pair, half, width = source_cache.shape
    steps = queries.shape[0]
    heads = fresh_cache.shape[3]
    asks = queries.shape[3] * steps
    exponents = jnp.arange(width // 2, dtype=F32) * (2.0 / width)
    frequency = jnp.power(F32(ROPE_BASE), -exponents)
    places = positions[0][:, None] + jnp.arange(8, dtype=jnp.int32)[None, :]
    angles = places.astype(F32)[..., None] * frequency
    turn = jnp.concatenate([jnp.cos(angles), jnp.sin(angles)], axis=-1)
    fresh = jnp.transpose(fresh_cache[:, 0], (1, 2, 3, 0, 4))
    fresh = jnp.pad(fresh, ((0, 0), (0, 0), (0, 0), (0, 8 - steps), (0, 0)))
    fresh = fresh.reshape(requests, heads * pair * 8, width)
    smem = pl.BlockSpec(memory_space=pltpu.SMEM)
    vmem = pl.BlockSpec(memory_space=pltpu.VMEM)
    dma = pltpu.SemaphoreType.DMA
    attended, scales = pl.pallas_call(
        functools.partial(kernel, n),
        out_shape=(
            jax.ShapeDtypeStruct(queries.shape, BF16),
            jax.ShapeDtypeStruct((requests, 16, width), BF16),
        ),
        in_specs=[smem] * 3 + [pl.BlockSpec(memory_space=pl.ANY)] + [vmem] * 3,
        out_specs=(vmem, vmem),
        scratch_shapes=[
            pltpu.VMEM((width, width), BF16),
            pltpu.VMEM((requests, heads, pair, half, width), BF16),
            pltpu.VMEM((requests, heads, pair, half, width), BF16),
            pltpu.VMEM((requests, heads, pair, 2 * half, width), BF16),
            pltpu.VMEM((requests, 16, width), F32),
            pltpu.VMEM((n, asks + 32, width), BF16),
            pltpu.VMEM((n, asks + 32, width), BF16),
            pltpu.VMEM((n, 8, width), F32),
            pltpu.VMEM((n, 8, width), F32),
            pltpu.VMEM((n, asks + 16, width), BF16),
            pltpu.VMEM((n, asks + 16, width), BF16),
            dma((3,)),
            dma((n,)),
            dma((n,)),
            dma((n,)),
            dma((n,)),
            dma((n,)),
            dma((n,)),
        ],
        compiler_params=pltpu.CompilerParams(
            collective_id=0, has_side_effects=True, vmem_limit_bytes=52 * 2**20
        ),
        cost_estimate=pl.CostEstimate(flops=10**9, bytes_accessed=4 * 10**6, transcendentals=10**5),
    )(block_table, lengths, target_map, source_cache, queries, fresh, turn)
    scales = scales[:, : heads * pair, 0].reshape(1, requests, heads, pair)
    return scales, attended


def solution(mesh):
    return jax.shard_map(
        on_device,
        mesh=mesh,
        in_specs=(
            P(("groups", "inst"), None, None, None, "tp", None),
            P(("groups", "inst"), None),
            P("groups", None),
            P("groups", None),
            P(None, ("groups", "inst"), None, "tp", None),
            P(None, ("groups", "inst"), None, "tp", None, None),
            P(("groups", "inst"), None),
        ),
        out_specs=(
            P(("groups", "inst"), None, "tp", None),
            P(None, ("groups", "inst"), None, "tp", None),
        ),
        check_vma=False,
    )
```

```python
import functools
import math

import jax
import jax.numpy as jnp
from jax import lax
from jax.experimental import pallas as pl
from jax.experimental.pallas import tpu as pltpu
from jax.sharding import PartitionSpec as P

ROPE_BASE = 1000000.0
MESH = pl.DeviceIdType.MESH
F32 = jnp.float32
BF16 = jnp.bfloat16


def sylvester(order):
    rows = lax.broadcasted_iota(jnp.int32, (order, order), 0)
    columns = lax.broadcasted_iota(jnp.int32, (order, order), 1)
    common = jnp.bitwise_and(rows, columns)
    parity = jnp.zeros((order, order), dtype=jnp.int32)
    for level in range(order.bit_length() - 1):
        parity = parity + jnp.bitwise_and(lax.shift_right_logical(common, level), 1)
    return (1 - 2 * jnp.bitwise_and(parity, 1)).astype(F32).astype(BF16)


def split(values):
    high = values.astype(BF16)
    low = (values - high.astype(F32)).astype(BF16)
    return high, low


def dot(a, b):
    return jnp.dot(a, b, preferred_element_type=F32)


def dot_t(a, b):
    return lax.dot_general(
        a, b, (((1,), (1,)), ((), ())), preferred_element_type=F32
    )


def kernel(
    n,
    table_hbm,
    length_hbm,
    map_hbm,
    cache_ref,
    query_hbm,
    fresh_ref,
    turn_ref,
    out_ref,
    scale_ref,
    table_ref,
    length_ref,
    map_ref,
    query_ref,
    had,
    own,
    other,
    quant,
    scale,
    ask,
    asked,
    turns,
    turned,
    reply,
    replied,
    swap_sem,
    ask_send,
    ask_recv,
    turn_send,
    turn_recv,
    reply_send,
    reply_recv,
):
    group = lax.axis_index("groups")
    me = lax.axis_index("inst")
    rank = lax.axis_index("tp")
    steps, _, requests, query_heads, width = query_ref.shape
    heads = cache_ref.shape[2] // 2
    half = cache_ref.shape[4]
    share = query_heads // heads
    rows = steps * share
    asks = heads * rows
    factor = 1.0 / math.sqrt(width)

    def after(d):
        return lax.rem(me + d, n)

    def before(d):
        return lax.rem(me + n - d, n)

    fetch = pltpu.make_async_copy(
        cache_ref.at[0, :, pl.ds(rank * heads, heads)], own, swap_sem.at[2]
    )
    fetch.start()
    plans = [
        pltpu.make_async_copy(map_hbm, map_ref, swap_sem.at[3]),
        pltpu.make_async_copy(table_hbm, table_ref, swap_sem.at[4]),
        pltpu.make_async_copy(length_hbm, length_ref, swap_sem.at[5]),
        pltpu.make_async_copy(query_hbm, query_ref, swap_sem.at[6]),
    ]
    for plan in plans:
        plan.start()
    barrier = pltpu.get_barrier_semaphore()

    pl.semaphore_signal(barrier, inc=1, device_id=(group, me, 1 - rank), device_id_type=MESH)

    @pl.loop(1, n)
    def _(d):
        pl.semaphore_signal(barrier, inc=1, device_id=(group, after(d), rank), device_id_type=MESH)

    had[...] = sylvester(width)
    plans[0].wait()
    plans[3].wait()

    @pl.loop(1, n)
    def _(d):
        source = after(d)
        chosen = jnp.int32(0)
        for j in range(requests):
            chosen = jnp.maximum(chosen, jnp.where(map_ref[source, j] == me, j, 0))
        for g in range(heads):
            for u in range(steps):
                ask[source, pl.ds(g * rows + u * share, share), :] = query_ref[
                    u, 0, chosen, pl.ds(g * share, share), :
                ]
        ask[source, pl.ds(asks, 32), :] = fresh_ref[chosen]
        turns[source] = turn_ref[chosen]

    pl.semaphore_wait(barrier, n)

    swap = pltpu.make_async_remote_copy(
        src_ref=cache_ref.at[0, :, pl.ds((1 - rank) * heads, heads)],
        dst_ref=other,
        send_sem=swap_sem.at[0],
        recv_sem=swap_sem.at[1],
        device_id=(group, me, 1 - rank),
        device_id_type=MESH,
    )
    swap.start()

    def ask_copy(d, slot, target):
        return pltpu.make_async_remote_copy(
            src_ref=ask.at[after(d)],
            dst_ref=asked.at[slot],
            send_sem=ask_send.at[d],
            recv_sem=ask_recv.at[d],
            device_id=(group, target, rank),
            device_id_type=MESH,
        )

    def turn_copy(d, slot, target):
        return pltpu.make_async_remote_copy(
            src_ref=turns.at[after(d)],
            dst_ref=turned.at[slot],
            send_sem=turn_send.at[d],
            recv_sem=turn_recv.at[d],
            device_id=(group, target, rank),
            device_id_type=MESH,
        )

    def reply_copy(d, slot, target):
        return pltpu.make_async_remote_copy(
            src_ref=reply.at[before(d)],
            dst_ref=replied.at[slot],
            send_sem=reply_send.at[d],
            recv_sem=reply_recv.at[d],
            device_id=(group, target, rank),
            device_id_type=MESH,
        )

    @pl.loop(1, n)
    def _(d):
        source = after(d)
        turn_copy(d, me, source).start()
        ask_copy(d, me, source).start()

    fetch.wait()
    plans[1].wait()
    plans[2].wait()
    swap.wait_recv()

    token = lax.broadcasted_iota(jnp.int32, (2 * half, width), 0)
    token = jnp.where(token < half, token + rank * half, token - half + (1 - rank) * half)
    line = lax.broadcasted_iota(jnp.int32, (16, width), 0)

    @pl.loop(0, requests)
    def _(j):
        page = table_ref[0, j]
        keep = token < length_ref[me, j]
        signs = had[...]
        packed = jnp.zeros((16, width), F32)
        for g in range(heads):
            for e in range(2):
                values = jnp.concatenate(
                    [own[page, g, e], other[page, g, e]], axis=0
                )
                rotated = jnp.where(keep, dot(values, signs) * factor, 0.0)
                top = jnp.max(jnp.max(jnp.abs(rotated), axis=0, keepdims=True), axis=1, keepdims=True)
                block = (jnp.broadcast_to(top, (16, width)) + 1e-06).astype(BF16).astype(F32)
                packed = jnp.where(line == 2 * g + e, block, packed)
                quant[j, g, e] = (rotated / block[:1]).astype(BF16)
        scale[j] = packed

    lane = lax.broadcasted_iota(jnp.int32, (8, width), 1)
    row = lax.broadcasted_iota(jnp.int32, (rows, width), 0)
    later = lax.broadcasted_iota(jnp.int32, (rows, width), 1)
    open_ = later * share <= row
    column = lax.broadcasted_iota(jnp.int32, (rows, 2 * half), 1)
    column = jnp.where(column < half, column + rank * half, column - half + (1 - rank) * half)

    def attend(target):
        chosen = jnp.int32(0)
        for j in range(requests):
            chosen = jnp.maximum(chosen, jnp.where(map_ref[me, j] == target, j, 0))
        keep = column < length_ref[me, chosen]
        signs = had[...]
        packed = scale[chosen]
        turn = turned[target]
        flipped = pltpu.roll(turn, width // 2, 1)
        cosine = jnp.where(lane < width // 2, turn, flipped)
        sine = jnp.where(lane < width // 2, -flipped, turn)

        def wide(values):
            blocks = [jnp.broadcast_to(values[u : u + 1], (share, width)) for u in range(steps)]
            return jnp.concatenate(blocks * heads, axis=0)

        fresh = asked[target, pl.ds(asks, 32), :].astype(F32)
        query = asked[target, pl.ds(0, asks), :].astype(F32)
        query = query * wide(cosine) + pltpu.roll(query, width // 2, 1) * wide(sine)
        high, low = split(query)
        query_high, query_low = split(dot(high, signs) + dot(low, signs))
        zeros = jnp.zeros((8, width), F32)
        blank = jnp.zeros((width - 16, width), BF16)
        results = []
        for g in range(heads):
            key = fresh[16 * g : 16 * g + 8]
            key = key * cosine + pltpu.roll(key, width // 2, 1) * sine
            high = key.astype(BF16).astype(F32)
            key = dot(jnp.concatenate([high, key - high], axis=0).astype(BF16), signs)
            key = key[:8] + key[8:]
            high = key.astype(BF16).astype(F32)
            key = jnp.concatenate([high, key - high], axis=0).astype(BF16)
            keys = jnp.concatenate([quant[chosen, g, 0], key, blank], axis=0)
            value = jnp.concatenate([fresh[16 * g + 8 : 16 * g + 16], zeros], axis=0).astype(BF16)
            value = jnp.concatenate([signs, value, blank], axis=0)
            mine = slice(g * rows, (g + 1) * rows)
            scores = dot_t(query_high[mine], keys) + dot_t(query_low[mine], keys)
            cached = scores[:, :width] * (packed[2 * g : 2 * g + 1] * (factor * factor))
            cached = jnp.where(keep, cached, -jnp.inf)
            recent = scores[:, width:]
            recent = (recent + pltpu.roll(recent, width - 8, 1)) * (factor * factor * factor)
            recent = jnp.where(open_, recent, -jnp.inf)
            top = jnp.max(jnp.maximum(cached, recent), axis=1, keepdims=True)
            cached = jnp.exp(cached - top).astype(BF16)
            recent = jnp.exp(recent - top).astype(BF16)
            total = jnp.sum(cached.astype(F32) + recent.astype(F32), axis=1, keepdims=True)
            mixed = dot(cached, quant[chosen, g, 1])
            mixed = (mixed * (packed[2 * g + 1 : 2 * g + 2] * factor)).astype(BF16)
            mixed = dot(jnp.concatenate([mixed, recent], axis=1), value)
            results.append((mixed / total).astype(BF16))
        results.append(packed.astype(BF16))
        return jnp.concatenate(results, axis=0)

    def serve(distances):
        for d in distances:
            turn_copy(d, before(d), before(d)).wait_recv()
            ask_copy(d, before(d), before(d)).wait_recv()
        results = [attend(before(d)) for d in distances]
        for d, result in zip(distances, results):
            reply[before(d)] = result
            reply_copy(d, me, before(d)).start()

    @pl.loop(1, n)
    def _(d):
        serve([d])

    @pl.loop(1, n)
    def _(d):
        source = after(d)
        reply_copy(d, source, source).wait_recv()

    @pl.loop(0, requests)
    def _(j):
        source = jnp.int32(0)
        for s in range(n):
            source = jnp.maximum(source, jnp.where(map_ref[s, j] == me, s, 0))
        for g in range(heads):
            for u in range(steps):
                out_ref[u, 0, j, pl.ds(g * share, share), :] = replied[
                    source, pl.ds(g * rows + u * share, share), :
                ]
        scale_ref[j] = replied[source, pl.ds(asks, 16), :]

    swap.wait_send()

    @pl.loop(1, n)
    def _(d):
        turn_copy(d, me, after(d)).wait_send()
        ask_copy(d, me, after(d)).wait_send()
        reply_copy(d, me, before(d)).wait_send()


def on_device(source_cache, block_table, lengths, target_map, queries, fresh_cache, positions):
    n = lax.axis_size("inst")
    _, requests, all_heads, pair, half, width = source_cache.shape
    steps = queries.shape[0]
    heads = fresh_cache.shape[3]
    asks = queries.shape[3] * steps
    exponents = jnp.arange(width // 2, dtype=F32) * (2.0 / width)
    frequency = jnp.power(F32(ROPE_BASE), -exponents)
    places = positions[0][:, None] + jnp.arange(8, dtype=jnp.int32)[None, :]
    angles = places.astype(F32)[..., None] * frequency
    turn = jnp.concatenate([jnp.cos(angles), jnp.sin(angles)], axis=-1)
    fresh = jnp.transpose(fresh_cache[:, 0], (1, 2, 3, 0, 4))
    fresh = jnp.pad(fresh, ((0, 0), (0, 0), (0, 0), (0, 8 - steps), (0, 0)))
    fresh = fresh.reshape(requests, heads * pair * 8, width)
    hbm = pl.BlockSpec(memory_space=pltpu.HBM)
    vmem = pl.BlockSpec(memory_space=pltpu.VMEM)
    dma = pltpu.SemaphoreType.DMA
    attended, scales = pl.pallas_call(
        functools.partial(kernel, n),
        out_shape=(
            jax.ShapeDtypeStruct(queries.shape, BF16),
            jax.ShapeDtypeStruct((requests, 16, width), BF16),
        ),
        in_specs=[hbm] * 5 + [vmem] * 2,
        out_specs=(vmem, vmem),
        scratch_shapes=[
            pltpu.SMEM(block_table.shape, jnp.int32),
            pltpu.SMEM(lengths.shape, jnp.int32),
            pltpu.SMEM(target_map.shape, jnp.int32),
            pltpu.VMEM(queries.shape, BF16),
            pltpu.VMEM((width, width), BF16),
            pltpu.VMEM((requests, heads, pair, half, width), BF16),
            pltpu.VMEM((requests, heads, pair, half, width), BF16),
            pltpu.VMEM((requests, heads, pair, 2 * half, width), BF16),
            pltpu.VMEM((requests, 16, width), F32),
            pltpu.VMEM((n, asks + 32, width), BF16),
            pltpu.VMEM((n, asks + 32, width), BF16),
            pltpu.VMEM((n, 8, width), F32),
            pltpu.VMEM((n, 8, width), F32),
            pltpu.VMEM((n, asks + 16, width), BF16),
            pltpu.VMEM((n, asks + 16, width), BF16),
            dma((7,)),
            dma((n,)),
            dma((n,)),
            dma((n,)),
            dma((n,)),
            dma((n,)),
            dma((n,)),
        ],
        compiler_params=pltpu.CompilerParams(
            collective_id=0, has_side_effects=True, vmem_limit_bytes=61 * 2**20
        ),
        cost_estimate=pl.CostEstimate(flops=10**9, bytes_accessed=4 * 10**6, transcendentals=10**5),
    )(block_table, lengths, target_map, source_cache, queries, fresh, turn)
    scales = scales[:, : heads * pair, 0].reshape(1, requests, heads, pair)
    return scales, attended


def solution(mesh):
    return jax.shard_map(
        on_device,
        mesh=mesh,
        in_specs=(
            P(("groups", "inst"), None, None, None, "tp", None),
            P(("groups", "inst"), None),
            P("groups", None),
            P("groups", None),
            P(None, ("groups", "inst"), None, "tp", None),
            P(None, ("groups", "inst"), None, "tp", None, None),
            P(("groups", "inst"), None),
        ),
        out_specs=(
            P(("groups", "inst"), None, "tp", None),
            P(None, ("groups", "inst"), None, "tp", None),
        ),
        check_vma=False,
    )
```

```python
import functools
import math

import jax
import jax.numpy as jnp
from jax import lax
from jax.experimental import pallas as pl
from jax.experimental.pallas import tpu as pltpu
from jax.sharding import PartitionSpec as P

ROPE_BASE = 1000000.0
MESH = pl.DeviceIdType.MESH
F32 = jnp.float32
BF16 = jnp.bfloat16


def sylvester(order):
    rows = lax.broadcasted_iota(jnp.int32, (order, order), 0)
    columns = lax.broadcasted_iota(jnp.int32, (order, order), 1)
    common = jnp.bitwise_and(rows, columns)
    parity = jnp.zeros((order, order), dtype=jnp.int32)
    for level in range(order.bit_length() - 1):
        parity = parity + jnp.bitwise_and(lax.shift_right_logical(common, level), 1)
    return (1 - 2 * jnp.bitwise_and(parity, 1)).astype(F32).astype(BF16)


def split(values):
    high = values.astype(BF16)
    low = (values - high.astype(F32)).astype(BF16)
    return high, low


def dot(a, b):
    return jnp.dot(a, b, preferred_element_type=F32)


def dot_t(a, b):
    return lax.dot_general(
        a, b, (((1,), (1,)), ((), ())), preferred_element_type=F32
    )


def kernel(
    n,
    table_hbm,
    length_hbm,
    map_hbm,
    cache_ref,
    query_hbm,
    fresh_ref,
    turn_ref,
    out_ref,
    scale_ref,
    table_ref,
    length_ref,
    map_ref,
    query_ref,
    had,
    own,
    other,
    quant,
    scale,
    ask,
    asked,
    turns,
    turned,
    reply,
    replied,
    swap_sem,
    ask_send,
    ask_recv,
    turn_send,
    turn_recv,
    reply_send,
    reply_recv,
):
    group = lax.axis_index("groups")
    me = lax.axis_index("inst")
    rank = lax.axis_index("tp")
    steps, _, requests, query_heads, width = query_ref.shape
    heads = cache_ref.shape[2] // 2
    half = cache_ref.shape[4]
    share = query_heads // heads
    rows = steps * share
    asks = heads * rows
    factor = 1.0 / math.sqrt(width)

    def after(d):
        return lax.rem(me + d, n)

    def before(d):
        return lax.rem(me + n - d, n)

    fetch = pltpu.make_async_copy(
        cache_ref.at[0, :, pl.ds(rank * heads, heads)], own, swap_sem.at[2]
    )
    fetch.start()
    plans = [
        pltpu.make_async_copy(map_hbm, map_ref, swap_sem.at[3]),
        pltpu.make_async_copy(table_hbm, table_ref, swap_sem.at[4]),
        pltpu.make_async_copy(length_hbm, length_ref, swap_sem.at[5]),
        pltpu.make_async_copy(query_hbm, query_ref, swap_sem.at[6]),
    ]
    for plan in plans:
        plan.start()
    barrier = pltpu.get_barrier_semaphore()

    pl.semaphore_signal(barrier, inc=1, device_id=(group, me, 1 - rank), device_id_type=MESH)

    @pl.loop(1, n)
    def _(d):
        pl.semaphore_signal(barrier, inc=1, device_id=(group, after(d), rank), device_id_type=MESH)

    had[...] = sylvester(width)
    plans[0].wait()
    plans[3].wait()

    @pl.loop(1, n)
    def _(d):
        source = after(d)
        chosen = jnp.int32(0)
        for j in range(requests):
            chosen = jnp.maximum(chosen, jnp.where(map_ref[source, j] == me, j, 0))
        for g in range(heads):
            for u in range(steps):
                ask[source, pl.ds(g * rows + u * share, share), :] = query_ref[
                    u, 0, chosen, pl.ds(g * share, share), :
                ]
        ask[source, pl.ds(asks, 32), :] = fresh_ref[chosen]
        turns[source] = turn_ref[chosen]

    pl.semaphore_wait(barrier, n)

    swap = pltpu.make_async_remote_copy(
        src_ref=cache_ref.at[0, :, pl.ds((1 - rank) * heads, heads)],
        dst_ref=other,
        send_sem=swap_sem.at[0],
        recv_sem=swap_sem.at[1],
        device_id=(group, me, 1 - rank),
        device_id_type=MESH,
    )
    swap.start()

    def ask_copy(d, slot, target):
        return pltpu.make_async_remote_copy(
            src_ref=ask.at[after(d)],
            dst_ref=asked.at[slot],
            send_sem=ask_send.at[d],
            recv_sem=ask_recv.at[d],
            device_id=(group, target, rank),
            device_id_type=MESH,
        )

    def turn_copy(d, slot, target):
        return pltpu.make_async_remote_copy(
            src_ref=turns.at[after(d)],
            dst_ref=turned.at[slot],
            send_sem=turn_send.at[d],
            recv_sem=turn_recv.at[d],
            device_id=(group, target, rank),
            device_id_type=MESH,
        )

    def reply_copy(d, slot, target):
        return pltpu.make_async_remote_copy(
            src_ref=reply.at[before(d)],
            dst_ref=replied.at[slot],
            send_sem=reply_send.at[d],
            recv_sem=reply_recv.at[d],
            device_id=(group, target, rank),
            device_id_type=MESH,
        )

    @pl.loop(1, n)
    def _(d):
        source = after(d)
        turn_copy(d, me, source).start()
        ask_copy(d, me, source).start()

    fetch.wait()
    plans[1].wait()
    plans[2].wait()
    swap.wait_recv()

    token = lax.broadcasted_iota(jnp.int32, (2 * half, width), 0)
    token = jnp.where(token < half, token + rank * half, token - half + (1 - rank) * half)
    line = lax.broadcasted_iota(jnp.int32, (16, width), 0)

    @pl.loop(0, requests)
    def _(j):
        page = table_ref[0, j]
        keep = token < length_ref[me, j]
        signs = had[...]
        packed = jnp.zeros((16, width), F32)
        for g in range(heads):
            for e in range(2):
                values = jnp.concatenate(
                    [own[page, g, e], other[page, g, e]], axis=0
                )
                rotated = jnp.where(keep, dot(values, signs) * factor, 0.0)
                top = jnp.max(jnp.max(jnp.abs(rotated), axis=0, keepdims=True), axis=1, keepdims=True)
                block = (jnp.broadcast_to(top, (16, width)) + 1e-06).astype(BF16).astype(F32)
                packed = jnp.where(line == 2 * g + e, block, packed)
                quant[j, g, e] = (rotated / block[:1]).astype(BF16)
        scale[j] = packed

    lane = lax.broadcasted_iota(jnp.int32, (8, width), 1)
    row = lax.broadcasted_iota(jnp.int32, (rows, width), 0)
    later = lax.broadcasted_iota(jnp.int32, (rows, width), 1)
    open_ = later * share <= row
    column = lax.broadcasted_iota(jnp.int32, (rows, 2 * half), 1)
    column = jnp.where(column < half, column + rank * half, column - half + (1 - rank) * half)

    def attend(target):
        chosen = jnp.int32(0)
        for j in range(requests):
            chosen = jnp.maximum(chosen, jnp.where(map_ref[me, j] == target, j, 0))
        keep = column < length_ref[me, chosen]
        signs = had[...]
        packed = scale[chosen]
        turn = turned[target]
        flipped = pltpu.roll(turn, width // 2, 1)
        cosine = jnp.where(lane < width // 2, turn, flipped)
        sine = jnp.where(lane < width // 2, -flipped, turn)

        def wide(values):
            blocks = [jnp.broadcast_to(values[u : u + 1], (share, width)) for u in range(steps)]
            return jnp.concatenate(blocks * heads, axis=0)

        fresh = asked[target, pl.ds(asks, 32), :].astype(F32)
        query = asked[target, pl.ds(0, asks), :].astype(F32)
        query = query * wide(cosine) + pltpu.roll(query, width // 2, 1) * wide(sine)
        high, low = split(query)
        query_high, query_low = split(dot(high, signs) + dot(low, signs))
        zeros = jnp.zeros((8, width), F32)
        blank = jnp.zeros((width - 16, width), BF16)
        results = []
        for g in range(heads):
            key = fresh[16 * g : 16 * g + 8]
            key = key * cosine + pltpu.roll(key, width // 2, 1) * sine
            high = key.astype(BF16).astype(F32)
            key = dot(jnp.concatenate([high, key - high], axis=0).astype(BF16), signs)
            key = key[:8] + key[8:]
            high = key.astype(BF16).astype(F32)
            key = jnp.concatenate([high, key - high], axis=0).astype(BF16)
            keys = jnp.concatenate([quant[chosen, g, 0], key, blank], axis=0)
            value = jnp.concatenate([fresh[16 * g + 8 : 16 * g + 16], zeros], axis=0).astype(BF16)
            value = jnp.concatenate([signs, value, blank], axis=0)
            mine = slice(g * rows, (g + 1) * rows)
            scores = dot_t(query_high[mine], keys) + dot_t(query_low[mine], keys)
            cached = scores[:, :width] * (packed[2 * g : 2 * g + 1] * (factor * factor))
            cached = jnp.where(keep, cached, -jnp.inf)
            recent = scores[:, width:]
            recent = (recent + pltpu.roll(recent, width - 8, 1)) * (factor * factor * factor)
            recent = jnp.where(open_, recent, -jnp.inf)
            top = jnp.max(jnp.maximum(cached, recent), axis=1, keepdims=True)
            cached = jnp.exp(cached - top).astype(BF16)
            recent = jnp.exp(recent - top).astype(BF16)
            total = jnp.sum(cached.astype(F32) + recent.astype(F32), axis=1, keepdims=True)
            mixed = dot(cached, quant[chosen, g, 1])
            mixed = (mixed * (packed[2 * g + 1 : 2 * g + 2] * factor)).astype(BF16)
            mixed = dot(jnp.concatenate([mixed, recent], axis=1), value)
            results.append((mixed / total).astype(BF16))
        results.append(packed.astype(BF16))
        return jnp.concatenate(results, axis=0)

    def serve(distances):
        for d in distances:
            turn_copy(d, before(d), before(d)).wait_recv()
            ask_copy(d, before(d), before(d)).wait_recv()
        results = [attend(before(d)) for d in distances]
        for d, result in zip(distances, results):
            reply[before(d)] = result
            reply_copy(d, me, before(d)).start()

    serve([1])

    @pl.loop(0, (n - 2) // 2)
    def _(pair):
        serve([2 + 2 * pair, 3 + 2 * pair])

    @pl.loop(1, n)
    def _(d):
        source = after(d)
        reply_copy(d, source, source).wait_recv()

    @pl.loop(0, requests)
    def _(j):
        source = jnp.int32(0)
        for s in range(n):
            source = jnp.maximum(source, jnp.where(map_ref[s, j] == me, s, 0))
        for g in range(heads):
            for u in range(steps):
                out_ref[u, 0, j, pl.ds(g * share, share), :] = replied[
                    source, pl.ds(g * rows + u * share, share), :
                ]
        scale_ref[j] = replied[source, pl.ds(asks, 16), :]

    swap.wait_send()

    @pl.loop(1, n)
    def _(d):
        turn_copy(d, me, after(d)).wait_send()
        ask_copy(d, me, after(d)).wait_send()
        reply_copy(d, me, before(d)).wait_send()


def on_device(source_cache, block_table, lengths, target_map, queries, fresh_cache, positions):
    n = lax.axis_size("inst")
    _, requests, all_heads, pair, half, width = source_cache.shape
    steps = queries.shape[0]
    heads = fresh_cache.shape[3]
    asks = queries.shape[3] * steps
    exponents = jnp.arange(width // 2, dtype=F32) * (2.0 / width)
    frequency = jnp.power(F32(ROPE_BASE), -exponents)
    places = positions[0][:, None] + jnp.arange(8, dtype=jnp.int32)[None, :]
    angles = places.astype(F32)[..., None] * frequency
    turn = jnp.concatenate([jnp.cos(angles), jnp.sin(angles)], axis=-1)
    fresh = jnp.transpose(fresh_cache[:, 0], (1, 2, 3, 0, 4))
    fresh = jnp.pad(fresh, ((0, 0), (0, 0), (0, 0), (0, 8 - steps), (0, 0)))
    fresh = fresh.reshape(requests, heads * pair * 8, width)
    hbm = pl.BlockSpec(memory_space=pltpu.HBM)
    vmem = pl.BlockSpec(memory_space=pltpu.VMEM)
    dma = pltpu.SemaphoreType.DMA
    attended, scales = pl.pallas_call(
        functools.partial(kernel, n),
        out_shape=(
            jax.ShapeDtypeStruct(queries.shape, BF16),
            jax.ShapeDtypeStruct((requests, 16, width), BF16),
        ),
        in_specs=[hbm] * 5 + [vmem] * 2,
        out_specs=(vmem, vmem),
        scratch_shapes=[
            pltpu.SMEM(block_table.shape, jnp.int32),
            pltpu.SMEM(lengths.shape, jnp.int32),
            pltpu.SMEM(target_map.shape, jnp.int32),
            pltpu.VMEM(queries.shape, BF16),
            pltpu.VMEM((width, width), BF16),
            pltpu.VMEM((requests, heads, pair, half, width), BF16),
            pltpu.VMEM((requests, heads, pair, half, width), BF16),
            pltpu.VMEM((requests, heads, pair, 2 * half, width), BF16),
            pltpu.VMEM((requests, 16, width), F32),
            pltpu.VMEM((n, asks + 32, width), BF16),
            pltpu.VMEM((n, asks + 32, width), BF16),
            pltpu.VMEM((n, 8, width), F32),
            pltpu.VMEM((n, 8, width), F32),
            pltpu.VMEM((n, asks + 16, width), BF16),
            pltpu.VMEM((n, asks + 16, width), BF16),
            dma((7,)),
            dma((n,)),
            dma((n,)),
            dma((n,)),
            dma((n,)),
            dma((n,)),
            dma((n,)),
        ],
        compiler_params=pltpu.CompilerParams(
            collective_id=0, has_side_effects=True, vmem_limit_bytes=53 * 2**20
        ),
        cost_estimate=pl.CostEstimate(flops=10**9, bytes_accessed=4 * 10**6, transcendentals=10**5),
    )(block_table, lengths, target_map, source_cache, queries, fresh, turn)
    scales = scales[:, : heads * pair, 0].reshape(1, requests, heads, pair)
    return scales, attended


def solution(mesh):
    return jax.shard_map(
        on_device,
        mesh=mesh,
        in_specs=(
            P(("groups", "inst"), None, None, None, "tp", None),
            P(("groups", "inst"), None),
            P("groups", None),
            P("groups", None),
            P(None, ("groups", "inst"), None, "tp", None),
            P(None, ("groups", "inst"), None, "tp", None, None),
            P(("groups", "inst"), None),
        ),
        out_specs=(
            P(("groups", "inst"), None, "tp", None),
            P(None, ("groups", "inst"), None, "tp", None),
        ),
        check_vma=False,
    )
```
